32 devices in a mesh: group: 2 (over y), hid: 16 (over z, x, core).
Axes of the slice: x: 2, y: 2, z: 4, core: 2. Of those that a mesh axis runs over, the one named last changes fastest.
Arguments:
- tokens: bfloat16 [64, 8192], P(('group', 'hid')), parts along dimension 0, may hold values from -48 to 48
- norm_gain: bfloat16 [8192], replicated, may hold values from 0.099609375 to 1.8984375
- curve_point: float32 [1], replicated, may hold values from 0.25 to 0.75
- gate_tiles: bfloat16 [3, 16, 36, 128, 128], P(None, 'hid'), may hold values from -0.1875 to 0.1875
- up_tiles: bfloat16 [3, 16, 36, 128, 128], P(None, 'hid'), may hold values from -0.1875 to 0.1875
- down_tiles: bfloat16 [3, 16, 36, 128, 128], P(None, 'hid'), may hold values from -0.375 to 0.375
- gate_index: int32 [3, 16, 36], P(None, 'hid'), may hold values from 0 to 63, as said below
- up_index: int32 [3, 16, 36], P(None, 'hid'), may hold values from 0 to 63, as said below
- down_index: int32 [3, 16, 36], P(None, 'hid'), may hold values from 0 to 63, as said below
- kept_counts: int32 [3, 3, 16], P(None, None, 'hid'), may hold values from 16 to 36, as said below
Outputs:
- ffn_out: bfloat16 [64, 8192], P(('group', 'hid')), parts along dimension 0
The draws below stay inside these ranges and needn't reach their ends.
There are 2 independent parts, one for each index of `group`. The reference program is written for one: setup_inputs(seed, part) draws one part's arguments, and reference() takes and returns one part's arrays. A program takes and returns all parts, laid end to end along the dimension named above; an argument that names none is the same for every part. Nothing has to cross between parts.
Inputs may be any that keep to these rules, and one draw needn't show every extreme that they name: `kept_counts`: for each matrix and control point, some hidden block column holds exactly 36 kept blocks; which column that is may differ from one matrix and control point to another. `gate_index`: the entries of one list are distinct; only the first kept_counts entries of a list name kept blocks, the others are ignored. `up_index`: as gate_index. `down_index`: as gate_index.
All inputs are finite; a program needn't handle non-finite values.
Results may differ from the reference program's by a relative error of at most 0.0064.
Values may be sent and summed in bfloat16 or wider, within the bound.
A program may use at most 128 MiB of HBM per device.

```python
import math
import jax
import jax.numpy as jnp
from jax import lax

D = 8192
BLK = 128
MAXB = 36
FF = 2048
RB = 64
HBLK = 16
KLO = 16
TOKENS = 32


def draw_tokens(key, part):
    key_base, key_rows, key_cols = jax.random.split(key, 3)
    row_scale = jnp.exp(jax.random.uniform(key_rows, (TOKENS, 1), jnp.float32, math.log(0.4), math.log(4.0)))
    col_scale = jnp.exp(jax.random.uniform(key_cols, (1, D), jnp.float32, math.log(0.4), math.log(4.0)))
    values = jax.random.truncated_normal(key_base, -3.0, 3.0, (TOKENS, D), jnp.float32) * row_scale * col_scale
    return values.astype(jnp.bfloat16)


def draw_lists(key, salt):
    list_keys = jax.random.split(jax.random.fold_in(key, salt), 3 * HBLK)
    lists = jax.vmap(lambda one_key: jax.random.permutation(one_key, RB)[:MAXB])(list_keys)
    return lists.reshape(3, HBLK, MAXB).astype(jnp.int32)


def draw_gate_index(key, part):
    return draw_lists(key, 11)


def draw_up_index(key, part):
    return draw_lists(key, 23)


def draw_down_index(key, part):
    return draw_lists(key, 37)


def draw_kept_counts(key, part):
    key_counts = jax.random.fold_in(key, 51)
    key_full = jax.random.fold_in(key, 67)
    counts = jax.random.randint(key_counts, (3, 3, HBLK), KLO, MAXB + 1)
    full_column = jax.random.randint(key_full, (3, 3, 1), 0, HBLK)
    columns = jnp.arange(HBLK, dtype=jnp.int32).reshape(1, 1, HBLK)
    return jnp.where(columns == full_column, MAXB, counts).astype(jnp.int32)


def level_of(stream_key, shape, pieces, low, top_value):
    level = 1.0
    for axis_at, parts in pieces:
        steps = jax.random.uniform(jax.random.fold_in(jax.random.fold_in(stream_key, 6), axis_at), (parts,), jnp.float32, low / len(pieces), top_value / len(pieces))
        level = level * jnp.repeat(jnp.exp(steps), shape[axis_at] // parts).reshape((-1,) + (1,) * (len(shape) - 1 - axis_at))
    return level


def noise(rng, shape, scale, limit, cuts=(), kind=jnp.bfloat16):
    values = scale * jax.random.normal(rng, shape, jnp.float32)
    if cuts:
        values = values * level_of(rng, shape, cuts, -0.22, 0.18)
    return jnp.clip(values, -limit, limit).astype(kind)


def setup_inputs(seed: int = 0, part: int = 0) -> dict:
    key_of = jax.random.split(jax.random.key(seed), 11)
    part_splits = jax.random.split(jax.random.fold_in(key_of[10], part), 11)
    return {
        "tokens": draw_tokens(jax.random.fold_in(jax.random.fold_in(key_of[10], part), 71), part),
        "norm_gain": jnp.clip(1.0 + 0.18 * jax.random.normal(key_of[1], (D,), jnp.float32), 0.099609375, 1.8984375).astype(jnp.bfloat16),
        "curve_point": jnp.clip(jax.random.uniform(key_of[2], (1,), jnp.float32, 0.25, 0.75), 0.25, 0.75),
        "gate_tiles": noise(key_of[3], (3, HBLK, MAXB, BLK, BLK), (D // 8) ** -0.5, 0.1875, ((1, 16),)),
        "up_tiles": noise(key_of[4], (3, HBLK, MAXB, BLK, BLK), (D // 8) ** -0.5, 0.1875, ((1, 16),)),
        "down_tiles": noise(key_of[5], (3, HBLK, MAXB, BLK, BLK), (FF // 8) ** -0.5, 0.375, ((1, 16),)),
        "gate_index": draw_gate_index(jax.random.fold_in(key_of[10], 71), part),
        "up_index": draw_up_index(jax.random.fold_in(key_of[10], 71), part),
        "down_index": draw_down_index(jax.random.fold_in(key_of[10], 71), part),
        "kept_counts": draw_kept_counts(jax.random.fold_in(key_of[10], 71), part),
    }


EPS = 1e-05

def place_tiles(tile_set, block_ids, kept, column_blocks):
    slot_ids = jnp.arange(tile_set.shape[0], dtype=jnp.int32)
    target = jnp.where(slot_ids < kept, block_ids, column_blocks).astype(jnp.int32)
    placed = jnp.zeros((column_blocks + 1,) + tile_set.shape[1:], tile_set.dtype)
    return placed.at[target].set(tile_set)[:column_blocks]

def reference(tokens, norm_gain, curve_point, gate_tiles, up_tiles, down_tiles, gate_index, up_index, down_index, kept_counts):
    column_blocks = D // BLK
    tokens_f32 = tokens.astype(jnp.float32)
    mean_square = lax.optimization_barrier(jnp.mean(tokens_f32 * tokens_f32, axis=-1, keepdims=True))
    normed = (tokens_f32 * lax.rsqrt(mean_square + EPS) * norm_gain.astype(jnp.float32)).astype(jnp.bfloat16)
    point = curve_point[0]
    blend_coef = ((1.0 - point) * (1.0 - point), 2.0 * point * (1.0 - point), point * point)
    row_count = normed.shape[0]

    def owner_step(running, owner_id):
        gate_sum = jnp.zeros((row_count, BLK), jnp.float32)
        up_sum = jnp.zeros((row_count, BLK), jnp.float32)
        for control in range(3):
            gate_panel = place_tiles(gate_tiles[control, owner_id], gate_index[control, owner_id], kept_counts[0, control, owner_id], column_blocks).reshape(D, BLK)
            up_panel = place_tiles(up_tiles[control, owner_id], up_index[control, owner_id], kept_counts[1, control, owner_id], column_blocks).reshape(D, BLK)
            gate_sum = gate_sum + blend_coef[control] * jnp.dot(normed, gate_panel, preferred_element_type=jnp.float32)
            up_sum = up_sum + blend_coef[control] * jnp.dot(normed, up_panel, preferred_element_type=jnp.float32)
        hidden = (jax.nn.silu(gate_sum) * up_sum).astype(jnp.bfloat16)
        down_sum = jnp.zeros((row_count, D), jnp.float32)
        for control in range(3):
            down_panel = place_tiles(down_tiles[control, owner_id], down_index[control, owner_id], kept_counts[2, control, owner_id], column_blocks)
            down_panel = down_panel.transpose(1, 0, 2).reshape(BLK, D)
            down_sum = down_sum + blend_coef[control] * jnp.dot(hidden, down_panel, preferred_element_type=jnp.float32)
        return (running + down_sum, None)
    total, _ = lax.scan(owner_step, jnp.zeros((row_count, D), jnp.float32), jnp.arange(FF // BLK, dtype=jnp.int32))
    return total.astype(jnp.bfloat16)
```

```python
import functools

import jax
import jax.numpy as jnp
from jax import lax
from jax.experimental import pallas as pl
from jax.experimental.pallas import tpu as pltpu
from jax.sharding import PartitionSpec as P

EPS = 1e-05
MESH = pl.DeviceIdType.MESH
F32 = jnp.float32
BF16 = jnp.bfloat16


def each(count, body):
    if count <= 8:
        for i in range(count):
            body(i)
    else:

        def step(i, carry):
            body(i)
            return carry

        lax.fori_loop(0, count, step, 0)


def kernel(
    n,
    chunks,
    tok,
    gain,
    point_ref,
    gate_idx,
    up_idx,
    down_idx,
    counts,
    gate_hbm,
    up_hbm,
    down_hbm,
    out,
    gate_w,
    up_w,
    down_w,
    gathered,
    stage,
    blocks,
    final,
    s1,
    r1,
    s2,
    r2,
    s3,
    r3,
    inv_v,
    inv_s,
    w_sem,
    inv_sem,
    ga_s,
    ga_r,
    gb_s,
    gb_r,
    gc_s,
    gc_r,
    s1_s,
    s1_r,
    s2_s,
    s2_r,
    s3_s,
    s3_r,
):
    rows, width = tok.shape
    blk = gate_w.shape[-1]
    nb = width // blk
    cap = gate_w.shape[1]
    msg = nb * rows
    part = msg // chunks
    na = n // 4
    half = n // 2

    h = lax.axis_index("hid")
    core = lax.rem(h, 2)
    b = lax.rem(h // 2, 2)
    a = h // 4

    def place(core_, b_, a_):
        return (core_ * 2 + b_) * na + a_

    def peer(a_, b_, core_):
        return {"hid": a_ * 4 + b_ * 2 + core_}

    core_peer = peer(a, b, 1 - core)
    b_peer = peer(a, 1 - b, core)
    me = place(core, b, a)

    def remote(src, dst, send, recv, to):
        return pltpu.make_async_remote_copy(
            src_ref=src, dst_ref=dst, send_sem=send, recv_sem=recv, device_id=to, device_id_type=MESH
        )

    loads = []
    for m, (src, dst) in enumerate(((gate_hbm, gate_w), (up_hbm, up_w))):
        for c in range(3):
            loads.append(pltpu.make_async_copy(src.at[c, 0], dst.at[c], w_sem.at[m, c]))
    for c in range(3):
        loads.append(
            pltpu.make_async_copy(down_hbm.at[c, 0], down_w.at[pl.ds(c * cap, cap)], w_sem.at[2, c])
        )
    for copy in loads:
        copy.start()

    barrier = pltpu.get_barrier_semaphore()

    def greet(i):
        to = peer(lax.rem(a + 1 + i, na), b, core)
        pl.semaphore_signal(barrier, inc=1, device_id=to, device_id_type=MESH)

    each(na - 1, greet)
    pl.semaphore_signal(barrier, inc=1, device_id=b_peer, device_id_type=MESH)
    pl.semaphore_signal(barrier, inc=1, device_id=core_peer, device_id_type=MESH)

    x = tok[...].astype(F32)
    mean_square = jnp.sum(x * x, axis=-1, keepdims=True) / width
    x = x * lax.rsqrt(mean_square + EPS) * gain[...].astype(F32)
    for r in range(nb):
        final[r * rows : (r + 1) * rows, :] = x[:, r * blk : (r + 1) * blk]
    gathered[me] = final[...].astype(BF16)

    pl.semaphore_wait(barrier, na + 1)

    def copy_a(i):
        blk_ref = gathered.at[me]
        return remote(blk_ref, blk_ref, ga_s.at[i], ga_r.at[i], peer(lax.rem(a + 1 + i, na), b, core))

    def copy_b(i):
        blk_ref = gathered.at[place(core, b, lax.rem(a - i + na, na))]
        return remote(blk_ref, blk_ref, gb_s.at[i], gb_r.at[i], b_peer)

    def copy_c(i, b_):
        at = place(core, b if b_ == 0 else 1 - b, lax.rem(a - i + na, na))
        blk_ref = gathered.at[at]
        sem = i + b_ * na
        return remote(blk_ref, blk_ref, gc_s.at[sem], gc_r.at[sem], core_peer)

    def got_a(i):
        ref = gathered.at[place(core, b, lax.rem(a - 1 - i + na, na))]
        remote(ref, ref, ga_s.at[i], ga_r.at[i], b_peer).wait_recv()

    def got_b(i):
        ref = gathered.at[place(core, 1 - b, lax.rem(a - i + na, na))]
        remote(ref, ref, gb_s.at[i], gb_r.at[i], b_peer).wait_recv()

    def got_c(i, b_):
        ref = gathered.at[place(1 - core, b if b_ == 0 else 1 - b, lax.rem(a - i + na, na))]
        sem = i + b_ * na
        remote(ref, ref, gc_s.at[sem], gc_r.at[sem], core_peer).wait_recv()

    copy_b(0).start()
    each(na - 1, lambda i: copy_a(i).start())
    copy_c(0, 0).start()

    zero_tile = 3 * cap
    lane = lax.broadcasted_iota(jnp.int32, (8, 128), 1)
    line = lax.broadcasted_iota(jnp.int32, (8, 128), 0)
    table = jnp.full((8, 128), zero_tile, jnp.int32)
    for c in range(3):
        kept = counts[2, c, 0]
        row = jnp.full((8, 128), zero_tile, jnp.int32)
        for s in range(cap):
            target = jnp.where(s < kept, down_idx[c, 0, s], -1)
            row = jnp.where(lane == target, c * cap + s, row)
        table = jnp.where(line == c, row, table)
    inv_v[...] = table
    inv_copy = pltpu.make_async_copy(inv_v, inv_s, inv_sem)
    inv_copy.start()
    blocks[nb] = jnp.zeros(blocks.shape[1:], BF16)
    down_w[zero_tile] = jnp.zeros((blk, blk), BF16)

    def on_a(i):
        got_a(i)
        copy_b(i + 1).start()
        copy_c(i + 1, 0).start()

    each(na - 1, on_a)

    def on_b(i):
        got_b(i)
        copy_c(i, 1).start()

    each(na, on_b)
    each(na, lambda i: got_c(i, 0))
    each(na, lambda i: got_c(i, 1))

    def widen(p):
        stage[pl.ds(p * msg, msg), :] = gathered[p].astype(F32)

    each(n, widen)

    def regroup(g):
        for d in range(8):
            r = g * 8 + d
            for t in range(rows):
                blocks[r, t * n : (t + 1) * n, :] = stage[pl.ds(r * rows + t, n, stride=msg), :].astype(BF16)

    each(nb // 8, regroup)

    point = point_ref[0]
    coef = ((1.0 - point) * (1.0 - point), 2.0 * point * (1.0 - point), point * point)

    def project(m, idx, w):
        total = jnp.zeros((rows * n, blk), F32)
        group = 12
        for c in range(3):
            loads[m * 3 + c].wait()
            kept = counts[m, c, 0]
            acc = jnp.zeros((rows * n, blk), F32)
            for g in range(0, cap, group):
                size = min(group, cap - g)
                left = jnp.concatenate(
                    [blocks[jnp.where(s < kept, idx[c, 0, s], nb)] for s in range(g, g + size)], axis=1
                )
                right = w[c, g : g + size].reshape(size * blk, blk)
                acc = acc + jnp.dot(left, right, preferred_element_type=F32)
            total = total + coef[c] * acc
        return total

    gate = project(0, gate_idx, gate_w)
    up = project(1, up_idx, up_w)
    hidden = (gate / (1.0 + jnp.exp(-gate)) * up).astype(BF16)

    for copy in loads[6:]:
        copy.wait()
    inv_copy.wait()

    per = nb // chunks

    def down(k):
        def some(g):
            for d in range(4):
                r = k * per + g * 4 + d
                total = jnp.zeros((rows * n, blk), F32)
                for c in range(3):
                    total = total + coef[c] * jnp.dot(hidden, down_w[inv_s[c, r]], preferred_element_type=F32)
                for t in range(rows):
                    stage[pl.ds(r * rows + t, n, stride=msg), :] = total[t * n : (t + 1) * n]

        each(per // 4, some)

    def piece(p, k):
        return stage[pl.ds(pl.multiple_of(p * msg + k * part, part), part), :]

    def send1(k):
        return remote(s1.at[k], r1.at[k], s1_s.at[k], s1_r.at[k], core_peer)

    def send2(k):
        return remote(s2.at[k], r2.at[k], s2_s.at[k], s2_r.at[k], b_peer)

    def send3(k, i):
        to = peer(lax.rem(a + 1 + i, na), b, core)
        return remote(s3.at[k, i], r3.at[k, i], s3_s.at[k, i], s3_r.at[k, i], to)

    def step1(k):
        down(k)

        def pack(q):
            s1[k, q] = piece((1 - core) * half + q, k).astype(BF16)

        each(half, pack)
        send1(k).start()

    def step2(k):
        send1(k).wait_recv()

        def pack(q):
            at = (1 - b) * na + q
            s2[k, q] = (piece(core * half + at, k) + r1[k, at].astype(F32)).astype(BF16)

        each(na, pack)
        send2(k).start()

    def step3(k):
        send2(k).wait_recv()

        def value(q):
            at = b * na + q
            return piece(core * half + at, k) + r1[k, at].astype(F32) + r2[k, q].astype(F32)

        def pack(i):
            s3[k, i] = value(lax.rem(a + 1 + i, na)).astype(BF16)
            send3(k, i).start()

        each(na - 1, pack)
        final[k * part : (k + 1) * part, :] = value(a)

    def step4(k):
        def add(i):
            send3(k, i).wait_recv()
            final[k * part : (k + 1) * part, :] += r3[k, i].astype(F32)

        each(na - 1, add)
        for r in range(k * per, (k + 1) * per):
            out[:, r * blk : (r + 1) * blk] = final[r * rows : (r + 1) * rows, :].astype(out.dtype)

    steps = (step1, step2, step3, step4)
    for tick in range(chunks + 3):
        for late, step in enumerate(steps):
            if 0 <= tick - late < chunks:
                step(tick - late)

    each(na - 1, lambda i: copy_a(i).wait_send())
    each(na, lambda i: copy_b(i).wait_send())
    each(na, lambda i: copy_c(i, 0).wait_send())
    each(na, lambda i: copy_c(i, 1).wait_send())
    for k in range(chunks):
        send1(k).wait_send()
        send2(k).wait_send()
        each(na - 1, lambda i: send3(k, i).wait_send())


def solution(mesh):
    n = mesh.shape["hid"]
    chunks = 4

    def shards(tokens, norm_gain, curve_point, gate_t, up_t, down_t, gate_i, up_i, down_i, counts):
        rows, width = tokens.shape
        cap, blk = gate_t.shape[2], gate_t.shape[-1]
        nb = width // blk
        msg = nb * rows
        part = msg // chunks
        na, half = n // 4, n // 2
        smem = pl.BlockSpec(memory_space=pltpu.SMEM)
        vmem = pl.BlockSpec(memory_space=pltpu.VMEM)
        hbm = pl.BlockSpec(memory_space=pl.ANY)
        dma = pltpu.SemaphoreType.DMA
        return pl.pallas_call(
            functools.partial(kernel, n, chunks),
            out_shape=jax.ShapeDtypeStruct((rows, width), BF16),
            in_specs=[vmem, vmem, smem, smem, smem, smem, smem, hbm, hbm, hbm],
            out_specs=vmem,
            scratch_shapes=[
                pltpu.VMEM((3, cap, blk, blk), BF16),
                pltpu.VMEM((3, cap, blk, blk), BF16),
                pltpu.VMEM((3 * cap + 1, blk, blk), BF16),
                pltpu.VMEM((n, msg, blk), BF16),
                pltpu.VMEM((n * msg, blk), F32),
                pltpu.VMEM((nb + 1, rows * n, blk), BF16),
                pltpu.VMEM((msg, blk), F32),
                pltpu.VMEM((chunks, half, part, blk), BF16),
                pltpu.VMEM((chunks, half, part, blk), BF16),
                pltpu.VMEM((chunks, na, part, blk), BF16),
                pltpu.VMEM((chunks, na, part, blk), BF16),
                pltpu.VMEM((chunks, na - 1, part, blk), BF16),
                pltpu.VMEM((chunks, na - 1, part, blk), BF16),
                pltpu.VMEM((8, 128), jnp.int32),
                pltpu.SMEM((8, 128), jnp.int32),
                dma((3, 3)),
                dma(()),
                dma((na - 1,)),
                dma((na - 1,)),
                dma((na,)),
                dma((na,)),
                dma((2 * na,)),
                dma((2 * na,)),
                dma((chunks,)),
                dma((chunks,)),
                dma((chunks,)),
                dma((chunks,)),
                dma((chunks, na - 1)),
                dma((chunks, na - 1)),
            ],
            compiler_params=pltpu.CompilerParams(
                collective_id=0, has_side_effects=True, vmem_limit_bytes=56 * 2**20
            ),
        )(
            tokens,
            norm_gain.reshape(1, width),
            curve_point,
            gate_i,
            up_i,
            down_i,
            counts,
            gate_t,
            up_t,
            down_t,
        )

    return jax.shard_map(
        shards,
        mesh=mesh,
        in_specs=(
            P(("group", "hid"), None),
            P(),
            P(),
            P(None, "hid", None, None, None),
            P(None, "hid", None, None, None),
            P(None, "hid", None, None, None),
            P(None, "hid", None),
            P(None, "hid", None),
            P(None, "hid", None),
            P(None, None, "hid"),
        ),
        out_specs=P(("group", "hid"), None),
        check_vma=False,
    )
```

```python
import functools

import jax
import jax.numpy as jnp
from jax import lax
from jax.experimental import pallas as pl
from jax.experimental.pallas import tpu as pltpu
from jax.sharding import PartitionSpec as P

EPS = 1e-05
MESH = pl.DeviceIdType.MESH
F32 = jnp.float32
BF16 = jnp.bfloat16


def each(count, body):
    if count <= 8:
        for i in range(count):
            body(i)
    else:

        def step(i, carry):
            body(i)
            return carry

        lax.fori_loop(0, count, step, 0)


def kernel(
    n,
    chunks,
    tok,
    gain,
    point_ref,
    gate_idx_hbm,
    up_idx_hbm,
    down_idx_hbm,
    counts_hbm,
    gate_hbm,
    up_hbm,
    down_hbm,
    out,
    gate_w,
    up_w,
    down_w,
    gathered,
    stage,
    blocks,
    final,
    s1,
    r1,
    s2,
    r2,
    s3,
    r3,
    gain_rows,
    gate_idx,
    up_idx,
    down_idx,
    counts,
    inv_v,
    inv_s,
    list_sem,
    w_sem,
    inv_sem,
    ga_s,
    ga_r,
    gb_s,
    gb_r,
    gc_s,
    gc_r,
    s1_s,
    s1_r,
    s2_s,
    s2_r,
    s3_s,
    s3_r,
):
    rows, width = tok.shape
    blk = gate_w.shape[-1]
    nb = width // blk
    cap = gate_w.shape[1]
    msg = nb * rows
    part = msg // chunks
    na = n // 4
    half = n // 2

    h = lax.axis_index("hid")
    core = lax.rem(h, 2)
    b = lax.rem(h // 2, 2)
    a = h // 4

    def place(core_, b_, a_):
        return (core_ * 2 + b_) * na + a_

    def peer(a_, b_, core_):
        return {"hid": a_ * 4 + b_ * 2 + core_}

    def near(i):
        total, bit = 0, 1
        while bit < na:
            total = total + lax.rem(a // bit + i // bit, 2) * bit
            bit *= 2
        return total

    core_peer = peer(a, b, 1 - core)
    b_peer = peer(a, 1 - b, core)
    me = place(core, b, a)

    def remote(src, dst, send, recv, to):
        return pltpu.make_async_remote_copy(
            src_ref=src, dst_ref=dst, send_sem=send, recv_sem=recv, device_id=to, device_id_type=MESH
        )

    lists = [
        pltpu.make_async_copy(src, dst, list_sem.at[i])
        for i, (src, dst) in enumerate(
            ((down_idx_hbm, down_idx), (counts_hbm, counts), (gate_idx_hbm, gate_idx), (up_idx_hbm, up_idx))
        )
    ]
    for copy in lists:
        copy.start()
    loads = []
    for m, (src, dst) in enumerate(((gate_hbm, gate_w), (up_hbm, up_w))):
        for c in range(3):
            loads.append(pltpu.make_async_copy(src.at[c, 0], dst.at[c], w_sem.at[m, c]))
    for c in range(3):
        loads.append(
            pltpu.make_async_copy(down_hbm.at[c, 0], down_w.at[pl.ds(c * cap, cap)], w_sem.at[2, c])
        )
    for copy in loads:
        copy.start()

    barrier = pltpu.get_barrier_semaphore()

    def greet(i):
        to = peer(near(i + 1), b, core)
        pl.semaphore_signal(barrier, inc=1, device_id=to, device_id_type=MESH)

    each(na - 1, greet)
    pl.semaphore_signal(barrier, inc=1, device_id=b_peer, device_id_type=MESH)
    pl.semaphore_signal(barrier, inc=1, device_id=core_peer, device_id_type=MESH)

    x = tok[...].astype(F32)
    mean_square = jnp.sum(x * x, axis=-1, keepdims=True) / width
    x = x * lax.rsqrt(mean_square + EPS)
    for r in range(nb):
        final[r * rows : (r + 1) * rows, :] = x[:, r * blk : (r + 1) * blk]
    for t in range(rows):
        gain_rows[pl.ds(t, nb, stride=rows), :] = gain[...].astype(F32)
    gathered[me] = (final[...] * gain_rows[...]).astype(BF16)

    pl.semaphore_wait(barrier, na + 1)

    def copy_a(i):
        blk_ref = gathered.at[me]
        return remote(blk_ref, blk_ref, ga_s.at[i], ga_r.at[i], peer(near(i + 1), b, core))

    def copy_b(i):
        blk_ref = gathered.at[place(core, b, near(i))]
        return remote(blk_ref, blk_ref, gb_s.at[i], gb_r.at[i], b_peer)

    def copy_c(i, b_):
        at = place(core, b if b_ == 0 else 1 - b, near(i))
        blk_ref = gathered.at[at]
        sem = i + b_ * na
        return remote(blk_ref, blk_ref, gc_s.at[sem], gc_r.at[sem], core_peer)

    def got_a(i):
        ref = gathered.at[place(core, b, near(i + 1))]
        remote(ref, ref, ga_s.at[i], ga_r.at[i], b_peer).wait_recv()

    def got_b(i):
        ref = gathered.at[place(core, 1 - b, near(i))]
        remote(ref, ref, gb_s.at[i], gb_r.at[i], b_peer).wait_recv()

    def got_c(i, b_):
        ref = gathered.at[place(1 - core, b if b_ == 0 else 1 - b, near(i))]
        sem = i + b_ * na
        remote(ref, ref, gc_s.at[sem], gc_r.at[sem], core_peer).wait_recv()

    copy_b(0).start()
    each(na - 1, lambda i: copy_a(i).start())
    copy_c(0, 0).start()

    zero_tile = 3 * cap
    for copy in lists[:2]:
        copy.wait()
    lane = lax.broadcasted_iota(jnp.int32, (8, 128), 1)
    line = lax.broadcasted_iota(jnp.int32, (8, 128), 0)
    table = jnp.full((8, 128), zero_tile, jnp.int32)
    for c in range(3):
        kept = counts[2, 0, c]
        row = jnp.full((8, 128), zero_tile, jnp.int32)
        for s in range(cap):
            target = jnp.where(s < kept, down_idx[c, 0, s], -1)
            row = jnp.where(lane == target, c * cap + s, row)
        table = jnp.where(line == c, row, table)
    inv_v[...] = table
    inv_copy = pltpu.make_async_copy(inv_v, inv_s, inv_sem)
    inv_copy.start()
    blocks[nb] = jnp.zeros(blocks.shape[1:], BF16)
    down_w[zero_tile] = jnp.zeros((blk, blk), BF16)

    def widen(p):
        stage[pl.ds(pl.multiple_of(p * msg, msg), msg), :] = gathered[p].astype(F32)

    widen(me)

    def on_a(i):
        got_a(i)
        copy_b(i + 1).start()
        copy_c(i + 1, 0).start()
        widen(place(core, b, near(i + 1)))

    each(na - 1, on_a)

    def on_b(i):
        got_b(i)
        copy_c(i, 1).start()
        widen(place(core, 1 - b, near(i)))

    each(na, on_b)

    def on_c(i, b_):
        got_c(i, b_)
        widen(place(1 - core, b if b_ == 0 else 1 - b, near(i)))

    each(na, lambda i: on_c(i, 0))
    each(na, lambda i: on_c(i, 1))

    def regroup(g):
        for d in range(8):
            r = g * 8 + d
            for t in range(rows):
                blocks[r, t * n : (t + 1) * n, :] = stage[pl.ds(r * rows + t, n, stride=msg), :].astype(BF16)

    each(nb // 8, regroup)

    point = point_ref[0]
    coef = ((1.0 - point) * (1.0 - point), 2.0 * point * (1.0 - point), point * point)

    for copy in lists[2:]:
        copy.wait()

    def project(m, idx, w):
        total = jnp.zeros((rows * n, blk), F32)
        group = 12
        for c in range(3):
            loads[m * 3 + c].wait()
            kept = counts[m, 0, c]
            acc = jnp.zeros((rows * n, blk), F32)
            for g in range(0, cap, group):
                size = min(group, cap - g)
                left = jnp.concatenate(
                    [blocks[jnp.where(s < kept, idx[c, 0, s], nb)] for s in range(g, g + size)], axis=1
                )
                right = w[c, g : g + size].reshape(size * blk, blk)
                acc = acc + jnp.dot(left, right, preferred_element_type=F32)
            total = total + coef[c] * acc
        return total

    gate = project(0, gate_idx, gate_w)
    up = project(1, up_idx, up_w)
    hidden = (gate / (1.0 + jnp.exp(-gate)) * up).astype(BF16)

    for copy in loads[6:]:
        copy.wait()
    inv_copy.wait()

    per = nb // chunks

    def down(k):
        def some(g):
            for d in range(4):
                r = k * per + g * 4 + d
                total = jnp.zeros((rows * n, blk), F32)
                for c in range(3):
                    total = total + coef[c] * jnp.dot(hidden, down_w[inv_s[c, r]], preferred_element_type=F32)
                for t in range(rows):
                    stage[pl.ds(r * rows + t, n, stride=msg), :] = total[t * n : (t + 1) * n]

        each(per // 4, some)

    def piece(p, k):
        return stage[pl.ds(pl.multiple_of(p * msg + k * part, part), part), :]

    def send1(k):
        return remote(s1.at[k], r1.at[k], s1_s.at[k], s1_r.at[k], core_peer)

    def send2(k):
        return remote(s2.at[k], r2.at[k], s2_s.at[k], s2_r.at[k], b_peer)

    def send3(k, i):
        to = peer(near(i + 1), b, core)
        return remote(s3.at[k, i], r3.at[k, i], s3_s.at[k, i], s3_r.at[k, i], to)

    def step1(k):
        down(k)

        def pack(q):
            s1[k, q] = piece((1 - core) * half + q, k).astype(BF16)

        each(half, pack)
        send1(k).start()

    def step2(k):
        send1(k).wait_recv()

        def pack(q):
            at = (1 - b) * na + q
            s2[k, q] = (piece(core * half + at, k) + r1[k, at].astype(F32)).astype(BF16)

        each(na, pack)
        send2(k).start()

    def step3(k):
        send2(k).wait_recv()

        def value(q):
            at = b * na + q
            return piece(core * half + at, k) + r1[k, at].astype(F32) + r2[k, q].astype(F32)

        def pack(i):
            s3[k, i] = value(near(i + 1)).astype(BF16)
            send3(k, i).start()

        each(na - 1, pack)
        final[k * part : (k + 1) * part, :] = value(a)

    def step4(k):
        def add(i):
            send3(k, i).wait_recv()
            final[k * part : (k + 1) * part, :] += r3[k, i].astype(F32)

        each(na - 1, add)
        for r in range(k * per, (k + 1) * per):
            out[:, r * blk : (r + 1) * blk] = final[r * rows : (r + 1) * rows, :].astype(out.dtype)

    for step in (step1, step2, step3, step4):
        for k in range(chunks):
            step(k)

    each(na - 1, lambda i: copy_a(i).wait_send())
    each(na, lambda i: copy_b(i).wait_send())
    each(na, lambda i: copy_c(i, 0).wait_send())
    each(na, lambda i: copy_c(i, 1).wait_send())
    for k in range(chunks):
        send1(k).wait_send()
        send2(k).wait_send()
        each(na - 1, lambda i: send3(k, i).wait_send())


def solution(mesh):
    n = mesh.shape["hid"]
    chunks = 4

    def shards(tokens, norm_gain, curve_point, gate_t, up_t, down_t, gate_i, up_i, down_i, counts):
        rows, width = tokens.shape
        cap, blk = gate_t.shape[2], gate_t.shape[-1]
        nb = width // blk
        msg = nb * rows
        part = msg // chunks
        na, half = n // 4, n // 2
        smem = pl.BlockSpec(memory_space=pltpu.SMEM)
        vmem = pl.BlockSpec(memory_space=pltpu.VMEM)
        hbm = pl.BlockSpec(memory_space=pl.ANY)
        dma = pltpu.SemaphoreType.DMA
        return pl.pallas_call(
            functools.partial(kernel, n, chunks),
            out_shape=jax.ShapeDtypeStruct((rows, width), BF16),
            in_specs=[vmem, vmem, smem] + [hbm] * 7,
            out_specs=vmem,
            scratch_shapes=[
                pltpu.VMEM((3, cap, blk, blk), BF16),
                pltpu.VMEM((3, cap, blk, blk), BF16),
                pltpu.VMEM((3 * cap + 1, blk, blk), BF16),
                pltpu.VMEM((n, msg, blk), BF16),
                pltpu.VMEM((n * msg, blk), F32),
                pltpu.VMEM((nb + 1, rows * n, blk), BF16),
                pltpu.VMEM((msg, blk), F32),
                pltpu.VMEM((chunks, half, part, blk), BF16),
                pltpu.VMEM((chunks, half, part, blk), BF16),
                pltpu.VMEM((chunks, na, part, blk), BF16),
                pltpu.VMEM((chunks, na, part, blk), BF16),
                pltpu.VMEM((chunks, na - 1, part, blk), BF16),
                pltpu.VMEM((chunks, na - 1, part, blk), BF16),
                pltpu.VMEM((msg, blk), F32),
                pltpu.SMEM(gate_i.shape, jnp.int32),
                pltpu.SMEM(up_i.shape, jnp.int32),
                pltpu.SMEM(down_i.shape, jnp.int32),
                pltpu.SMEM((3, 1, 3), jnp.int32),
                pltpu.VMEM((8, 128), jnp.int32),
                pltpu.SMEM((8, 128), jnp.int32),
                dma((4,)),
                dma((3, 3)),
                dma(()),
                dma((na - 1,)),
                dma((na - 1,)),
                dma((na,)),
                dma((na,)),
                dma((2 * na,)),
                dma((2 * na,)),
                dma((chunks,)),
                dma((chunks,)),
                dma((chunks,)),
                dma((chunks,)),
                dma((chunks, na - 1)),
                dma((chunks, na - 1)),
            ],
            compiler_params=pltpu.CompilerParams(
                collective_id=0, has_side_effects=True, vmem_limit_bytes=56 * 2**20
            ),
        )(
            tokens,
            norm_gain.reshape(nb, blk),
            curve_point,
            gate_i,
            up_i,
            down_i,
            jnp.transpose(counts, (0, 2, 1)),
            gate_t,
            up_t,
            down_t,
        )

    return jax.shard_map(
        shards,
        mesh=mesh,
        in_specs=(
            P(("group", "hid"), None),
            P(),
            P(),
            P(None, "hid", None, None, None),
            P(None, "hid", None, None, None),
            P(None, "hid", None, None, None),
            P(None, "hid", None),
            P(None, "hid", None),
            P(None, "hid", None),
            P(None, None, "hid"),
        ),
        out_specs=P(("group", "hid"), None),
        check_vma=False,
    )
```

```python
import functools

import jax
import jax.numpy as jnp
from jax import lax
from jax.experimental import pallas as pl
from jax.experimental.pallas import tpu as pltpu
from jax.sharding import PartitionSpec as P

EPS = 1e-05
MESH = pl.DeviceIdType.MESH
F32 = jnp.float32
BF16 = jnp.bfloat16


def each(count, body):
    if count <= 8:
        for i in range(count):
            body(i)
    else:

        def step(i, carry):
            body(i)
            return carry

        lax.fori_loop(0, count, step, 0)


def kernel(
    n,
    chunks,
    tok_hbm,
    gain_hbm,
    point_ref,
    gate_idx_hbm,
    up_idx_hbm,
    down_idx_hbm,
    counts_hbm,
    gate_hbm,
    up_hbm,
    down_hbm,
    out,
    gate_w,
    up_w,
    down_w,
    gathered,
    stage,
    blocks,
    final,
    s1,
    r1,
    s2,
    r2,
    s3,
    r3,
    tok,
    gain,
    gain_rows,
    gate_idx,
    up_idx,
    down_idx,
    counts,
    inv_v,
    inv_s,
    list_sem,
    tok_sem,
    w_sem,
    inv_sem,
    ga_s,
    ga_r,
    gb_s,
    gb_r,
    gc_s,
    gc_r,
    s1_s,
    s1_r,
    s2_s,
    s2_r,
    s3_s,
    s3_r,
):
    rows, width = tok.shape
    blk = gate_w.shape[-1]
    nb = width // blk
    cap = gate_w.shape[1]
    msg = nb * rows
    part = msg // chunks
    na = n // 4
    half = n // 2

    h = lax.axis_index("hid")
    core = lax.rem(h, 2)
    b = lax.rem(h // 2, 2)
    a = h // 4

    def place(core_, b_, a_):
        return (core_ * 2 + b_) * na + a_

    def peer(a_, b_, core_):
        return {"hid": a_ * 4 + b_ * 2 + core_}

    def near(i):
        total, bit = 0, 1
        while bit < na:
            total = total + lax.rem(a // bit + i // bit, 2) * bit
            bit *= 2
        return total

    core_peer = peer(a, b, 1 - core)
    b_peer = peer(a, 1 - b, core)
    me = place(core, b, a)

    def remote(src, dst, send, recv, to):
        return pltpu.make_async_remote_copy(
            src_ref=src, dst_ref=dst, send_sem=send, recv_sem=recv, device_id=to, device_id_type=MESH
        )

    early = [
        pltpu.make_async_copy(tok_hbm, tok, tok_sem.at[0]),
        pltpu.make_async_copy(gain_hbm, gain, tok_sem.at[1]),
    ]
    for copy in early:
        copy.start()

    barrier = pltpu.get_barrier_semaphore()

    def greet(i):
        to = peer(near(i + 1), b, core)
        pl.semaphore_signal(barrier, inc=1, device_id=to, device_id_type=MESH)

    each(na - 1, greet)
    pl.semaphore_signal(barrier, inc=1, device_id=b_peer, device_id_type=MESH)
    pl.semaphore_signal(barrier, inc=1, device_id=core_peer, device_id_type=MESH)

    lists = [
        pltpu.make_async_copy(src, dst, list_sem.at[i])
        for i, (src, dst) in enumerate(
            ((down_idx_hbm, down_idx), (counts_hbm, counts), (gate_idx_hbm, gate_idx), (up_idx_hbm, up_idx))
        )
    ]
    for copy in lists:
        copy.start()
    loads = []
    for m, (src, dst) in enumerate(((gate_hbm, gate_w), (up_hbm, up_w))):
        for c in range(3):
            loads.append(pltpu.make_async_copy(src.at[c, 0], dst.at[c], w_sem.at[m, c]))
    for c in range(3):
        loads.append(
            pltpu.make_async_copy(down_hbm.at[c, 0], down_w.at[pl.ds(c * cap, cap)], w_sem.at[2, c])
        )
    for copy in loads:
        copy.start()

    for copy in early:
        copy.wait()

    x = tok[...].astype(F32)
    mean_square = jnp.sum(x * x, axis=-1, keepdims=True) / width
    x = x * lax.rsqrt(mean_square + EPS)
    for r in range(nb):
        final[r * rows : (r + 1) * rows, :] = x[:, r * blk : (r + 1) * blk]
    for t in range(rows):
        gain_rows[pl.ds(t, nb, stride=rows), :] = gain[...].astype(F32)
    gathered[me] = (final[...] * gain_rows[...]).astype(BF16)

    pl.semaphore_wait(barrier, na + 1)

    def copy_a(i):
        blk_ref = gathered.at[me]
        return remote(blk_ref, blk_ref, ga_s.at[i], ga_r.at[i], peer(near(i + 1), b, core))

    def copy_b(i):
        blk_ref = gathered.at[place(core, b, near(i))]
        return remote(blk_ref, blk_ref, gb_s.at[i], gb_r.at[i], b_peer)

    def copy_c(i, b_):
        at = place(core, b if b_ == 0 else 1 - b, near(i))
        blk_ref = gathered.at[at]
        sem = i + b_ * na
        return remote(blk_ref, blk_ref, gc_s.at[sem], gc_r.at[sem], core_peer)

    def got_a(i):
        ref = gathered.at[place(core, b, near(i + 1))]
        remote(ref, ref, ga_s.at[i], ga_r.at[i], b_peer).wait_recv()

    def got_b(i):
        ref = gathered.at[place(core, 1 - b, near(i))]
        remote(ref, ref, gb_s.at[i], gb_r.at[i], b_peer).wait_recv()

    def got_c(i, b_):
        ref = gathered.at[place(1 - core, b if b_ == 0 else 1 - b, near(i))]
        sem = i + b_ * na
        remote(ref, ref, gc_s.at[sem], gc_r.at[sem], core_peer).wait_recv()

    copy_b(0).start()
    each(na - 1, lambda i: copy_a(i).start())
    copy_c(0, 0).start()

    zero_tile = 3 * cap
    for copy in lists[:2]:
        copy.wait()
    lane = lax.broadcasted_iota(jnp.int32, (8, 128), 1)
    line = lax.broadcasted_iota(jnp.int32, (8, 128), 0)
    table = jnp.full((8, 128), zero_tile, jnp.int32)
    for c in range(3):
        kept = counts[2, 0, c]
        row = jnp.full((8, 128), zero_tile, jnp.int32)
        for s in range(cap):
            target = jnp.where(s < kept, down_idx[c, 0, s], -1)
            row = jnp.where(lane == target, c * cap + s, row)
        table = jnp.where(line == c, row, table)
    inv_v[...] = table
    inv_copy = pltpu.make_async_copy(inv_v, inv_s, inv_sem)
    inv_copy.start()
    blocks[nb] = jnp.zeros(blocks.shape[1:], BF16)
    down_w[zero_tile] = jnp.zeros((blk, blk), BF16)

    def widen(p):
        stage[pl.ds(pl.multiple_of(p * msg, msg), msg), :] = gathered[p].astype(F32)

    widen(me)

    def on_a(i):
        got_a(i)
        copy_b(i + 1).start()
        copy_c(i + 1, 0).start()
        widen(place(core, b, near(i + 1)))

    each(na - 1, on_a)

    def on_b(i):
        got_b(i)
        copy_c(i, 1).start()
        widen(place(core, 1 - b, near(i)))

    each(na, on_b)

    def on_c(i, b_):
        got_c(i, b_)
        widen(place(1 - core, b if b_ == 0 else 1 - b, near(i)))

    each(na, lambda i: on_c(i, 0))
    each(na, lambda i: on_c(i, 1))

    def regroup(g):
        for d in range(8):
            r = g * 8 + d
            for t in range(rows):
                blocks[r, t * n : (t + 1) * n, :] = stage[pl.ds(r * rows + t, n, stride=msg), :].astype(BF16)

    each(nb // 8, regroup)

    point = point_ref[0]
    coef = ((1.0 - point) * (1.0 - point), 2.0 * point * (1.0 - point), point * point)

    for copy in lists[2:]:
        copy.wait()

    def project(m, idx, w):
        total = jnp.zeros((rows * n, blk), F32)
        group = 12
        for c in range(3):
            loads[m * 3 + c].wait()
            kept = counts[m, 0, c]
            acc = jnp.zeros((rows * n, blk), F32)
            for g in range(0, cap, group):
                size = min(group, cap - g)
                left = jnp.concatenate(
                    [blocks[jnp.where(s < kept, idx[c, 0, s], nb)] for s in range(g, g + size)], axis=1
                )
                right = w[c, g : g + size].reshape(size * blk, blk)
                acc = acc + jnp.dot(left, right, preferred_element_type=F32)
            total = total + coef[c] * acc
        return total

    gate = project(0, gate_idx, gate_w)
    up = project(1, up_idx, up_w)
    hidden = (gate / (1.0 + jnp.exp(-gate)) * up).astype(BF16)

    for copy in loads[6:]:
        copy.wait()
    inv_copy.wait()

    per = nb // chunks

    def down(k):
        def some(g):
            for d in range(4):
                r = k * per + g * 4 + d
                total = jnp.zeros((rows * n, blk), F32)
                for c in range(3):
                    total = total + coef[c] * jnp.dot(hidden, down_w[inv_s[c, r]], preferred_element_type=F32)
                for t in range(rows):
                    stage[pl.ds(r * rows + t, n, stride=msg), :] = total[t * n : (t + 1) * n]

        each(per // 4, some)

    def piece(p, k):
        return stage[pl.ds(pl.multiple_of(p * msg + k * part, part), part), :]

    def send1(k):
        return remote(s1.at[k], r1.at[k], s1_s.at[k], s1_r.at[k], core_peer)

    def send2(k):
        return remote(s2.at[k], r2.at[k], s2_s.at[k], s2_r.at[k], b_peer)

    def send3(k, i):
        to = peer(near(i + 1), b, core)
        return remote(s3.at[k, i], r3.at[k, i], s3_s.at[k, i], s3_r.at[k, i], to)

    def step1(k):
        down(k)

        def pack(q):
            s1[k, q] = piece((1 - core) * half + q, k).astype(BF16)

        each(half, pack)
        send1(k).start()

    def step2(k):
        send1(k).wait_recv()

        def pack(q):
            at = (1 - b) * na + q
            s2[k, q] = (piece(core * half + at, k) + r1[k, at].astype(F32)).astype(BF16)

        each(na, pack)
        send2(k).start()

    def step3(k):
        send2(k).wait_recv()

        def value(q):
            at = b * na + q
            return piece(core * half + at, k) + r1[k, at].astype(F32) + r2[k, q].astype(F32)

        def pack(i):
            s3[k, i] = value(near(i + 1)).astype(BF16)
            send3(k, i).start()

        each(na - 1, pack)
        final[k * part : (k + 1) * part, :] = value(a)

    def step4(k):
        def add(i):
            send3(k, i).wait_recv()
            final[k * part : (k + 1) * part, :] += r3[k, i].astype(F32)

        each(na - 1, add)
        for r in range(k * per, (k + 1) * per):
            out[:, r * blk : (r + 1) * blk] = final[r * rows : (r + 1) * rows, :].astype(out.dtype)

    for step in (step1, step2, step3, step4):
        for k in range(chunks):
            step(k)

    each(na - 1, lambda i: copy_a(i).wait_send())
    each(na, lambda i: copy_b(i).wait_send())
    each(na, lambda i: copy_c(i, 0).wait_send())
    each(na, lambda i: copy_c(i, 1).wait_send())
    for k in range(chunks):
        send1(k).wait_send()
        send2(k).wait_send()
        each(na - 1, lambda i: send3(k, i).wait_send())


def solution(mesh):
    n = mesh.shape["hid"]
    chunks = 4

    def shards(tokens, norm_gain, curve_point, gate_t, up_t, down_t, gate_i, up_i, down_i, counts):
        rows, width = tokens.shape
        cap, blk = gate_t.shape[2], gate_t.shape[-1]
        nb = width // blk
        msg = nb * rows
        part = msg // chunks
        na, half = n // 4, n // 2
        smem = pl.BlockSpec(memory_space=pltpu.SMEM)
        vmem = pl.BlockSpec(memory_space=pltpu.VMEM)
        hbm = pl.BlockSpec(memory_space=pl.ANY)
        dma = pltpu.SemaphoreType.DMA
        return pl.pallas_call(
            functools.partial(kernel, n, chunks),
            out_shape=jax.ShapeDtypeStruct((rows, width), BF16),
            in_specs=[hbm, hbm, smem] + [hbm] * 7,
            out_specs=vmem,
            scratch_shapes=[
                pltpu.VMEM((3, cap, blk, blk), BF16),
                pltpu.VMEM((3, cap, blk, blk), BF16),
                pltpu.VMEM((3 * cap + 1, blk, blk), BF16),
                pltpu.VMEM((n, msg, blk), BF16),
                pltpu.VMEM((n * msg, blk), F32),
                pltpu.VMEM((nb + 1, rows * n, blk), BF16),
                pltpu.VMEM((msg, blk), F32),
                pltpu.VMEM((chunks, half, part, blk), BF16),
                pltpu.VMEM((chunks, half, part, blk), BF16),
                pltpu.VMEM((chunks, na, part, blk), BF16),
                pltpu.VMEM((chunks, na, part, blk), BF16),
                pltpu.VMEM((chunks, na - 1, part, blk), BF16),
                pltpu.VMEM((chunks, na - 1, part, blk), BF16),
                pltpu.VMEM((rows, width), BF16),
                pltpu.VMEM((nb, blk), BF16),
                pltpu.VMEM((msg, blk), F32),
                pltpu.SMEM(gate_i.shape, jnp.int32),
                pltpu.SMEM(up_i.shape, jnp.int32),
                pltpu.SMEM(down_i.shape, jnp.int32),
                pltpu.SMEM((3, 1, 3), jnp.int32),
                pltpu.VMEM((8, 128), jnp.int32),
                pltpu.SMEM((8, 128), jnp.int32),
                dma((4,)),
                dma((2,)),
                dma((3, 3)),
                dma(()),
                dma((na - 1,)),
                dma((na - 1,)),
                dma((na,)),
                dma((na,)),
                dma((2 * na,)),
                dma((2 * na,)),
                dma((chunks,)),
                dma((chunks,)),
                dma((chunks,)),
                dma((chunks,)),
                dma((chunks, na - 1)),
                dma((chunks, na - 1)),
            ],
            compiler_params=pltpu.CompilerParams(
                collective_id=0, has_side_effects=True, vmem_limit_bytes=56 * 2**20
            ),
        )(
            tokens,
            norm_gain.reshape(nb, blk),
            curve_point,
            gate_i,
            up_i,
            down_i,
            jnp.transpose(counts, (0, 2, 1)),
            gate_t,
            up_t,
            down_t,
        )

    return jax.shard_map(
        shards,
        mesh=mesh,
        in_specs=(
            P(("group", "hid"), None),
            P(),
            P(),
            P(None, "hid", None, None, None),
            P(None, "hid", None, None, None),
            P(None, "hid", None, None, None),
            P(None, "hid", None),
            P(None, "hid", None),
            P(None, "hid", None),
            P(None, None, "hid"),
        ),
        out_specs=P(("group", "hid"), None),
        check_vma=False,
    )
```

```python
import functools

import jax
import jax.numpy as jnp
from jax import lax
from jax.experimental import pallas as pl
from jax.experimental.pallas import tpu as pltpu
from jax.sharding import PartitionSpec as P

EPS = 1e-05
MESH = pl.DeviceIdType.MESH
F32 = jnp.float32
BF16 = jnp.bfloat16


def each(count, body):
    if count <= 8:
        for i in range(count):
            body(i)
    else:

        def step(i, carry):
            body(i)
            return carry

        lax.fori_loop(0, count, step, 0)


def kernel(
    n,
    chunks,
    tok_hbm,
    gain_hbm,
    point_ref,
    gate_idx_hbm,
    up_idx_hbm,
    down_idx_hbm,
    counts_hbm,
    gate_hbm,
    up_hbm,
    down_hbm,
    out,
    gate_w,
    up_w,
    down_w,
    gathered,
    stage,
    blocks,
    final,
    s1,
    r1,
    s2,
    r2,
    s3,
    r3,
    tok,
    gain,
    gain_rows,
    gate_idx,
    up_idx,
    down_idx,
    counts,
    inv_v,
    inv_s,
    list_sem,
    tok_sem,
    w_sem,
    inv_sem,
    ga_s,
    ga_r,
    gb_s,
    gb_r,
    gc_s,
    gc_r,
    s1_s,
    s1_r,
    s2_s,
    s2_r,
    s3_s,
    s3_r,
):
    rows, width = tok.shape
    blk = gate_w.shape[-1]
    nb = width // blk
    cap = gate_w.shape[1]
    msg = nb * rows
    part = msg // chunks
    na = n // 4
    half = n // 2

    h = lax.axis_index("hid")
    core = lax.rem(h, 2)
    b = lax.rem(h // 2, 2)
    a = h // 4

    def place(core_, b_, a_):
        return (core_ * 2 + b_) * na + a_

    def peer(a_, b_, core_):
        return {"hid": a_ * 4 + b_ * 2 + core_}

    def near(i):
        total, bit = 0, 1
        while bit < na:
            total = total + lax.rem(a // bit + i // bit, 2) * bit
            bit *= 2
        return total

    core_peer = peer(a, b, 1 - core)
    b_peer = peer(a, 1 - b, core)
    me = place(core, b, a)

    def remote(src, dst, send, recv, to):
        return pltpu.make_async_remote_copy(
            src_ref=src, dst_ref=dst, send_sem=send, recv_sem=recv, device_id=to, device_id_type=MESH
        )

    early = [
        pltpu.make_async_copy(tok_hbm, tok, tok_sem.at[0]),
        pltpu.make_async_copy(gain_hbm, gain, tok_sem.at[1]),
    ]
    for copy in early:
        copy.start()

    barrier = pltpu.get_barrier_semaphore()

    def greet(i):
        to = peer(near(i + 1), b, core)
        pl.semaphore_signal(barrier, inc=1, device_id=to, device_id_type=MESH)

    each(na - 1, greet)
    pl.semaphore_signal(barrier, inc=1, device_id=b_peer, device_id_type=MESH)
    pl.semaphore_signal(barrier, inc=1, device_id=core_peer, device_id_type=MESH)

    lists = [
        pltpu.make_async_copy(src, dst, list_sem.at[i])
        for i, (src, dst) in enumerate(
            ((down_idx_hbm, down_idx), (counts_hbm, counts), (gate_idx_hbm, gate_idx), (up_idx_hbm, up_idx))
        )
    ]
    for copy in lists:
        copy.start()
    loads = []
    for m, (src, dst) in enumerate(((gate_hbm, gate_w), (up_hbm, up_w))):
        for c in range(3):
            loads.append(pltpu.make_async_copy(src.at[c, 0], dst.at[c], w_sem.at[m, c]))
    for c in range(3):
        loads.append(
            pltpu.make_async_copy(down_hbm.at[c, 0], down_w.at[pl.ds(c * cap, cap)], w_sem.at[2, c])
        )
    for copy in loads:
        copy.start()

    for copy in early:
        copy.wait()

    x = tok[...].astype(F32)
    mean_square = jnp.sum(x * x, axis=-1, keepdims=True) / width
    x = x * lax.rsqrt(mean_square + EPS)
    for r in range(nb):
        final[r * rows : (r + 1) * rows, :] = x[:, r * blk : (r + 1) * blk]
    for t in range(rows):
        gain_rows[pl.ds(t, nb, stride=rows), :] = gain[...].astype(F32)
    gathered[me] = (final[...] * gain_rows[...]).astype(BF16)

    pl.semaphore_wait(barrier, na + 1)

    def copy_a(i):
        blk_ref = gathered.at[me]
        return remote(blk_ref, blk_ref, ga_s.at[i], ga_r.at[i], peer(near(i + 1), b, core))

    def copy_b(i):
        blk_ref = gathered.at[place(core, b, near(i))]
        return remote(blk_ref, blk_ref, gb_s.at[i], gb_r.at[i], b_peer)

    def copy_c(i, b_):
        at = place(core, b if b_ == 0 else 1 - b, near(i))
        blk_ref = gathered.at[at]
        sem = i + b_ * na
        return remote(blk_ref, blk_ref, gc_s.at[sem], gc_r.at[sem], core_peer)

    def got_a(i):
        ref = gathered.at[place(core, b, near(i + 1))]
        remote(ref, ref, ga_s.at[i], ga_r.at[i], b_peer).wait_recv()

    def got_b(i):
        ref = gathered.at[place(core, 1 - b, near(i))]
        remote(ref, ref, gb_s.at[i], gb_r.at[i], b_peer).wait_recv()

    def got_c(i, b_):
        ref = gathered.at[place(1 - core, b if b_ == 0 else 1 - b, near(i))]
        sem = i + b_ * na
        remote(ref, ref, gc_s.at[sem], gc_r.at[sem], core_peer).wait_recv()

    copy_b(0).start()
    each(na - 1, lambda i: copy_a(i).start())
    copy_c(0, 0).start()

    zero_tile = 3 * cap
    for copy in lists[:2]:
        copy.wait()
    lane = lax.broadcasted_iota(jnp.int32, (8, 128), 1)
    line = lax.broadcasted_iota(jnp.int32, (8, 128), 0)
    table = jnp.full((8, 128), zero_tile, jnp.int32)
    for c in range(3):
        kept = counts[2, 0, c]
        row = jnp.full((8, 128), zero_tile, jnp.int32)
        for s in range(cap):
            target = jnp.where(s < kept, down_idx[c, 0, s], -1)
            row = jnp.where(lane == target, c * cap + s, row)
        table = jnp.where(line == c, row, table)
    inv_v[...] = table
    inv_copy = pltpu.make_async_copy(inv_v, inv_s, inv_sem)
    inv_copy.start()
    blocks[nb] = jnp.zeros(blocks.shape[1:], BF16)
    down_w[zero_tile] = jnp.zeros((blk, blk), BF16)

    def widen(p):
        stage[pl.ds(pl.multiple_of(p * msg, msg), msg), :] = gathered[p].astype(F32)

    widen(me)

    def on_a(i):
        got_a(i)
        copy_b(i + 1).start()
        copy_c(i + 1, 0).start()
        widen(place(core, b, near(i + 1)))

    each(na - 1, on_a)

    def on_b(i):
        got_b(i)
        copy_c(i, 1).start()
        widen(place(core, 1 - b, near(i)))

    each(na, on_b)

    def on_c(i, b_):
        got_c(i, b_)
        widen(place(1 - core, b if b_ == 0 else 1 - b, near(i)))

    each(na, lambda i: on_c(i, 0))
    each(na, lambda i: on_c(i, 1))

    def regroup(g):
        for d in range(8):
            r = g * 8 + d
            for t in range(rows):
                blocks[r, t * n : (t + 1) * n, :] = stage[pl.ds(r * rows + t, n, stride=msg), :].astype(BF16)

    each(nb // 8, regroup)

    point = point_ref[0]
    coef = ((1.0 - point) * (1.0 - point), 2.0 * point * (1.0 - point), point * point)

    for copy in lists[2:]:
        copy.wait()

    def project(m, idx, w):
        total = jnp.zeros((rows * n, blk), F32)
        group = 12
        for c in range(3):
            loads[m * 3 + c].wait()
            kept = counts[m, 0, c]
            acc = jnp.zeros((rows * n, blk), F32)
            for g in range(0, cap, group):
                size = min(group, cap - g)
                left = jnp.concatenate(
                    [blocks[jnp.where(s < kept, idx[c, 0, s], nb)] for s in range(g, g + size)], axis=1
                )
                right = w[c, g : g + size].reshape(size * blk, blk)
                acc = acc + jnp.dot(left, right, preferred_element_type=F32)
            total = total + coef[c] * acc
        return total

    gate = project(0, gate_idx, gate_w)
    up = project(1, up_idx, up_w)
    hidden = (gate / (1.0 + jnp.exp(-gate)) * up).astype(BF16)

    for copy in loads[6:]:
        copy.wait()
    inv_copy.wait()

    per = nb // chunks

    def down(k):
        def some(g):
            for d in range(4):
                r = k * per + g * 4 + d
                total = jnp.zeros((rows * n, blk), F32)
                for c in range(3):
                    total = total + coef[c] * jnp.dot(hidden, down_w[inv_s[c, r]], preferred_element_type=F32)
                for t in range(rows):
                    stage[pl.ds(r * rows + t, n, stride=msg), :] = total[t * n : (t + 1) * n]

        each(per // 4, some)

    def piece(p, k):
        return stage[pl.ds(pl.multiple_of(p * msg + k * part, part), part), :]

    def send1(k):
        return remote(s1.at[k], r1.at[k], s1_s.at[k], s1_r.at[k], core_peer)

    def send2(k):
        return remote(s2.at[k], r2.at[k], s2_s.at[k], s2_r.at[k], b_peer)

    def send3(k, i):
        to = peer(near(i + 1), b, core)
        return remote(s3.at[k, i], r3.at[k, i], s3_s.at[k, i], s3_r.at[k, i], to)

    def step1(k):
        down(k)

        def pack(q):
            s1[k, q] = piece((1 - core) * half + q, k).astype(BF16)

        each(half, pack)
        send1(k).start()

    def step2(k):
        send1(k).wait_recv()

        def pack(q):
            at = (1 - b) * na + q
            s2[k, q] = (piece(core * half + at, k) + r1[k, at].astype(F32)).astype(BF16)

        each(na, pack)
        send2(k).start()

    def step3(k):
        send2(k).wait_recv()

        def value(q):
            at = b * na + q
            return piece(core * half + at, k) + r1[k, at].astype(F32) + r2[k, q].astype(F32)

        def pack(i):
            s3[k, i] = value(near(i + 1)).astype(BF16)
            send3(k, i).start()

        each(na - 1, pack)
        final[k * part : (k + 1) * part, :] = value(a)

    def step4(k):
        def add(i):
            send3(k, i).wait_recv()
            final[k * part : (k + 1) * part, :] += r3[k, i].astype(F32)

        each(na - 1, add)
        for r in range(k * per, (k + 1) * per):
            out[:, r * blk : (r + 1) * blk] = final[r * rows : (r + 1) * rows, :].astype(out.dtype)

    for k in range(chunks + 1):
        if k < chunks:
            step1(k)
        if k >= 1:
            step2(k - 1)
    for step in (step3, step4):
        for k in range(chunks):
            step(k)

    each(na - 1, lambda i: copy_a(i).wait_send())
    each(na, lambda i: copy_b(i).wait_send())
    each(na, lambda i: copy_c(i, 0).wait_send())
    each(na, lambda i: copy_c(i, 1).wait_send())
    for k in range(chunks):
        send1(k).wait_send()
        send2(k).wait_send()
        each(na - 1, lambda i: send3(k, i).wait_send())


def solution(mesh):
    n = mesh.shape["hid"]
    chunks = 4

    def shards(tokens, norm_gain, curve_point, gate_t, up_t, down_t, gate_i, up_i, down_i, counts):
        rows, width = tokens.shape
        cap, blk = gate_t.shape[2], gate_t.shape[-1]
        nb = width // blk
        msg = nb * rows
        part = msg // chunks
        na, half = n // 4, n // 2
        smem = pl.BlockSpec(memory_space=pltpu.SMEM)
        vmem = pl.BlockSpec(memory_space=pltpu.VMEM)
        hbm = pl.BlockSpec(memory_space=pl.ANY)
        dma = pltpu.SemaphoreType.DMA
        return pl.pallas_call(
            functools.partial(kernel, n, chunks),
            out_shape=jax.ShapeDtypeStruct((rows, width), BF16),
            in_specs=[hbm, hbm, smem] + [hbm] * 7,
            out_specs=vmem,
            scratch_shapes=[
                pltpu.VMEM((3, cap, blk, blk), BF16),
                pltpu.VMEM((3, cap, blk, blk), BF16),
                pltpu.VMEM((3 * cap + 1, blk, blk), BF16),
                pltpu.VMEM((n, msg, blk), BF16),
                pltpu.VMEM((n * msg, blk), F32),
                pltpu.VMEM((nb + 1, rows * n, blk), BF16),
                pltpu.VMEM((msg, blk), F32),
                pltpu.VMEM((chunks, half, part, blk), BF16),
                pltpu.VMEM((chunks, half, part, blk), BF16),
                pltpu.VMEM((chunks, na, part, blk), BF16),
                pltpu.VMEM((chunks, na, part, blk), BF16),
                pltpu.VMEM((chunks, na - 1, part, blk), BF16),
                pltpu.VMEM((chunks, na - 1, part, blk), BF16),
                pltpu.VMEM((rows, width), BF16),
                pltpu.VMEM((nb, blk), BF16),
                pltpu.VMEM((msg, blk), F32),
                pltpu.SMEM(gate_i.shape, jnp.int32),
                pltpu.SMEM(up_i.shape, jnp.int32),
                pltpu.SMEM(down_i.shape, jnp.int32),
                pltpu.SMEM((3, 1, 3), jnp.int32),
                pltpu.VMEM((8, 128), jnp.int32),
                pltpu.SMEM((8, 128), jnp.int32),
                dma((4,)),
                dma((2,)),
                dma((3, 3)),
                dma(()),
                dma((na - 1,)),
                dma((na - 1,)),
                dma((na,)),
                dma((na,)),
                dma((2 * na,)),
                dma((2 * na,)),
                dma((chunks,)),
                dma((chunks,)),
                dma((chunks,)),
                dma((chunks,)),
                dma((chunks, na - 1)),
                dma((chunks, na - 1)),
            ],
            compiler_params=pltpu.CompilerParams(
                collective_id=0, has_side_effects=True, vmem_limit_bytes=56 * 2**20
            ),
        )(
            tokens,
            norm_gain.reshape(nb, blk),
            curve_point,
            gate_i,
            up_i,
            down_i,
            jnp.transpose(counts, (0, 2, 1)),
            gate_t,
            up_t,
            down_t,
        )

    return jax.shard_map(
        shards,
        mesh=mesh,
        in_specs=(
            P(("group", "hid"), None),
            P(),
            P(),
            P(None, "hid", None, None, None),
            P(None, "hid", None, None, None),
            P(None, "hid", None, None, None),
            P(None, "hid", None),
            P(None, "hid", None),
            P(None, "hid", None),
            P(None, None, "hid"),
        ),
        out_specs=P(("group", "hid"), None),
        check_vma=False,
    )
```

```python
import functools

import jax
import jax.numpy as jnp
from jax import lax
from jax.experimental import pallas as pl
from jax.experimental.pallas import tpu as pltpu
from jax.sharding import PartitionSpec as P

EPS = 1e-05
MESH = pl.DeviceIdType.MESH
F32 = jnp.float32
BF16 = jnp.bfloat16


def each(count, body):
    if count <= 8:
        for i in range(count):
            body(i)
    else:

        def step(i, carry):
            body(i)
            return carry

        lax.fori_loop(0, count, step, 0)


def kernel(
    n,
    chunks,
    tok_hbm,
    gain_hbm,
    point_ref,
    gate_idx_hbm,
    up_idx_hbm,
    down_idx_hbm,
    counts_hbm,
    gate_hbm,
    up_hbm,
    down_hbm,
    out,
    gate_w,
    up_w,
    down_w,
    gathered,
    stage,
    blocks,
    final,
    s1,
    r1,
    s2,
    r2,
    s3,
    r3,
    tok,
    gain,
    gain_rows,
    gate_idx,
    up_idx,
    down_idx,
    counts,
    inv_v,
    inv_s,
    list_sem,
    tok_sem,
    w_sem,
    inv_sem,
    ga_s,
    ga_r,
    gb_s,
    gb_r,
    gc_s,
    gc_r,
    s1_s,
    s1_r,
    s2_s,
    s2_r,
    s3_s,
    s3_r,
):
    rows, width = tok.shape
    blk = gate_w.shape[-1]
    nb = width // blk
    cap = gate_w.shape[1]
    msg = nb * rows
    part = msg // chunks
    na = n // 4
    half = n // 2

    h = lax.axis_index("hid")
    core = lax.rem(h, 2)
    b = lax.rem(h // 2, 2)
    a = h // 4

    def place(core_, b_, a_):
        return (core_ * 2 + b_) * na + a_

    def peer(a_, b_, core_):
        return {"hid": a_ * 4 + b_ * 2 + core_}

    def near(i):
        total, bit = 0, 1
        while bit < na:
            total = total + lax.rem(a // bit + i // bit, 2) * bit
            bit *= 2
        return total

    core_peer = peer(a, b, 1 - core)
    b_peer = peer(a, 1 - b, core)
    me = place(core, b, a)

    def remote(src, dst, send, recv, to):
        return pltpu.make_async_remote_copy(
            src_ref=src, dst_ref=dst, send_sem=send, recv_sem=recv, device_id=to, device_id_type=MESH
        )

    early = [
        pltpu.make_async_copy(tok_hbm, tok, tok_sem.at[0]),
        pltpu.make_async_copy(gain_hbm, gain, tok_sem.at[1]),
    ]
    for copy in early:
        copy.start()

    barrier = pltpu.get_barrier_semaphore()

    def greet(i):
        to = peer(near(i + 1), b, core)
        pl.semaphore_signal(barrier, inc=1, device_id=to, device_id_type=MESH)

    each(na - 1, greet)
    pl.semaphore_signal(barrier, inc=1, device_id=b_peer, device_id_type=MESH)
    pl.semaphore_signal(barrier, inc=1, device_id=core_peer, device_id_type=MESH)

    lists = [
        pltpu.make_async_copy(src, dst, list_sem.at[i])
        for i, (src, dst) in enumerate(
            ((down_idx_hbm, down_idx), (counts_hbm, counts), (gate_idx_hbm, gate_idx), (up_idx_hbm, up_idx))
        )
    ]
    for copy in lists:
        copy.start()
    loads = []
    for m, (src, dst) in enumerate(((gate_hbm, gate_w), (up_hbm, up_w))):
        for c in range(3):
            loads.append(pltpu.make_async_copy(src.at[c, 0], dst.at[c], w_sem.at[m, c]))
    for c in range(3):
        loads.append(
            pltpu.make_async_copy(down_hbm.at[c, 0], down_w.at[pl.ds(c * cap, cap)], w_sem.at[2, c])
        )
    for copy in loads:
        copy.start()

    for copy in early:
        copy.wait()

    x = tok[...].astype(F32)
    mean_square = jnp.sum(x * x, axis=-1, keepdims=True) / width
    x = x * lax.rsqrt(mean_square + EPS)
    for r in range(nb):
        final[r * rows : (r + 1) * rows, :] = x[:, r * blk : (r + 1) * blk]
    for t in range(rows):
        gain_rows[pl.ds(t, nb, stride=rows), :] = gain[...].astype(F32)
    gathered[me] = (final[...] * gain_rows[...]).astype(BF16)

    pl.semaphore_wait(barrier, na + 1)

    def copy_a(i):
        blk_ref = gathered.at[me]
        return remote(blk_ref, blk_ref, ga_s.at[i], ga_r.at[i], peer(near(i + 1), b, core))

    def copy_b(i):
        blk_ref = gathered.at[place(core, b, near(i))]
        return remote(blk_ref, blk_ref, gb_s.at[i], gb_r.at[i], b_peer)

    def copy_c(i, b_):
        at = place(core, b if b_ == 0 else 1 - b, near(i))
        blk_ref = gathered.at[at]
        sem = i + b_ * na
        return remote(blk_ref, blk_ref, gc_s.at[sem], gc_r.at[sem], core_peer)

    def got_a(i):
        ref = gathered.at[place(core, b, near(i + 1))]
        remote(ref, ref, ga_s.at[i], ga_r.at[i], b_peer).wait_recv()

    def got_b(i):
        ref = gathered.at[place(core, 1 - b, near(i))]
        remote(ref, ref, gb_s.at[i], gb_r.at[i], b_peer).wait_recv()

    def got_c(i, b_):
        ref = gathered.at[place(1 - core, b if b_ == 0 else 1 - b, near(i))]
        sem = i + b_ * na
        remote(ref, ref, gc_s.at[sem], gc_r.at[sem], core_peer).wait_recv()

    copy_b(0).start()
    each(na - 1, lambda i: copy_a(i).start())
    copy_c(0, 0).start()

    zero_tile = 3 * cap
    for copy in lists[:2]:
        copy.wait()
    lane = lax.broadcasted_iota(jnp.int32, (8, 128), 1)
    line = lax.broadcasted_iota(jnp.int32, (8, 128), 0)
    table = jnp.full((8, 128), zero_tile, jnp.int32)
    for c in range(3):
        kept = counts[2, 0, c]
        row = jnp.full((8, 128), zero_tile, jnp.int32)
        for s in range(cap):
            target = jnp.where(s < kept, down_idx[c, 0, s], -1)
            row = jnp.where(lane == target, c * cap + s, row)
        table = jnp.where(line == c, row, table)
    inv_v[...] = table
    inv_copy = pltpu.make_async_copy(inv_v, inv_s, inv_sem)
    inv_copy.start()
    blocks[nb] = jnp.zeros(blocks.shape[1:], BF16)
    down_w[zero_tile] = jnp.zeros((blk, blk), BF16)

    def widen(p):
        stage[pl.ds(pl.multiple_of(p * msg, msg), msg), :] = gathered[p].astype(F32)

    widen(me)

    def on_a(i):
        got_a(i)
        copy_b(i + 1).start()
        copy_c(i + 1, 0).start()
        widen(place(core, b, near(i + 1)))

    each(na - 1, on_a)

    def on_b(i):
        got_b(i)
        copy_c(i, 1).start()
        widen(place(core, 1 - b, near(i)))

    each(na, on_b)

    def on_c(i, b_):
        got_c(i, b_)
        widen(place(1 - core, b if b_ == 0 else 1 - b, near(i)))

    each(na, lambda i: on_c(i, 0))
    each(na, lambda i: on_c(i, 1))

    def regroup(g):
        for d in range(8):
            r = g * 8 + d
            for t in range(rows):
                blocks[r, t * n : (t + 1) * n, :] = stage[pl.ds(r * rows + t, n, stride=msg), :].astype(BF16)

    each(nb // 8, regroup)

    point = point_ref[0]
    coef = ((1.0 - point) * (1.0 - point), 2.0 * point * (1.0 - point), point * point)

    for copy in lists[2:]:
        copy.wait()

    def project(m, idx, w):
        total = jnp.zeros((rows * n, blk), F32)
        group = 12
        for c in range(3):
            loads[m * 3 + c].wait()
            kept = counts[m, 0, c]
            acc = jnp.zeros((rows * n, blk), F32)
            for g in range(0, cap, group):
                size = min(group, cap - g)
                left = jnp.concatenate(
                    [blocks[jnp.where(s < kept, idx[c, 0, s], nb)] for s in range(g, g + size)], axis=1
                )
                right = w[c, g : g + size].reshape(size * blk, blk)
                acc = acc + jnp.dot(left, right, preferred_element_type=F32)
            total = total + coef[c] * acc
        return total

    gate = project(0, gate_idx, gate_w)
    up = project(1, up_idx, up_w)
    hidden = (gate / (1.0 + jnp.exp(-gate)) * up).astype(BF16)

    for copy in loads[6:]:
        copy.wait()
    inv_copy.wait()

    per = nb // chunks

    def down(k):
        def some(g):
            first = k * per + g * 4
            total = jnp.zeros((rows * n, 4 * blk), F32)
            for c in range(3):
                tiles = jnp.concatenate([down_w[inv_s[c, first + d]] for d in range(4)], axis=1)
                total = total + coef[c] * jnp.dot(hidden, tiles, preferred_element_type=F32)
            for d in range(4):
                for t in range(rows):
                    stage[pl.ds((first + d) * rows + t, n, stride=msg), :] = total[
                        t * n : (t + 1) * n, d * blk : (d + 1) * blk
                    ]

        each(per // 4, some)

    def piece(p, k):
        return stage[pl.ds(pl.multiple_of(p * msg + k * part, part), part), :]

    def send1(k):
        return remote(s1.at[k], r1.at[k], s1_s.at[k], s1_r.at[k], core_peer)

    def send2(k):
        return remote(s2.at[k], r2.at[k], s2_s.at[k], s2_r.at[k], b_peer)

    def send3(k, i):
        to = peer(near(i + 1), b, core)
        return remote(s3.at[k, i], r3.at[k, i], s3_s.at[k, i], s3_r.at[k, i], to)

    def step1(k):
        down(k)

        def pack(q):
            s1[k, q] = piece((1 - core) * half + q, k).astype(BF16)

        each(half, pack)
        send1(k).start()

    def step2(k):
        send1(k).wait_recv()

        def pack(q):
            at = (1 - b) * na + q
            s2[k, q] = (piece(core * half + at, k) + r1[k, at].astype(F32)).astype(BF16)

        each(na, pack)
        send2(k).start()

    def step3(k):
        send2(k).wait_recv()

        def value(q):
            at = b * na + q
            return piece(core * half + at, k) + r1[k, at].astype(F32) + r2[k, q].astype(F32)

        def pack(i):
            s3[k, i] = value(near(i + 1)).astype(BF16)
            send3(k, i).start()

        each(na - 1, pack)
        final[k * part : (k + 1) * part, :] = value(a)

    def step4(k):
        def add(i):
            send3(k, i).wait_recv()
            final[k * part : (k + 1) * part, :] += r3[k, i].astype(F32)

        each(na - 1, add)
        for r in range(k * per, (k + 1) * per):
            out[:, r * blk : (r + 1) * blk] = final[r * rows : (r + 1) * rows, :].astype(out.dtype)

    for step in (step1, step2, step3, step4):
        for k in range(chunks):
            step(k)

    each(na - 1, lambda i: copy_a(i).wait_send())
    each(na, lambda i: copy_b(i).wait_send())
    each(na, lambda i: copy_c(i, 0).wait_send())
    each(na, lambda i: copy_c(i, 1).wait_send())
    for k in range(chunks):
        send1(k).wait_send()
        send2(k).wait_send()
        each(na - 1, lambda i: send3(k, i).wait_send())


def solution(mesh):
    n = mesh.shape["hid"]
    chunks = 4

    def shards(tokens, norm_gain, curve_point, gate_t, up_t, down_t, gate_i, up_i, down_i, counts):
        rows, width = tokens.shape
        cap, blk = gate_t.shape[2], gate_t.shape[-1]
        nb = width // blk
        msg = nb * rows
        part = msg // chunks
        na, half = n // 4, n // 2
        smem = pl.BlockSpec(memory_space=pltpu.SMEM)
        vmem = pl.BlockSpec(memory_space=pltpu.VMEM)
        hbm = pl.BlockSpec(memory_space=pl.ANY)
        dma = pltpu.SemaphoreType.DMA
        return pl.pallas_call(
            functools.partial(kernel, n, chunks),
            out_shape=jax.ShapeDtypeStruct((rows, width), BF16),
            in_specs=[hbm, hbm, smem] + [hbm] * 7,
            out_specs=vmem,
            scratch_shapes=[
                pltpu.VMEM((3, cap, blk, blk), BF16),
                pltpu.VMEM((3, cap, blk, blk), BF16),
                pltpu.VMEM((3 * cap + 1, blk, blk), BF16),
                pltpu.VMEM((n, msg, blk), BF16),
                pltpu.VMEM((n * msg, blk), F32),
                pltpu.VMEM((nb + 1, rows * n, blk), BF16),
                pltpu.VMEM((msg, blk), F32),
                pltpu.VMEM((chunks, half, part, blk), BF16),
                pltpu.VMEM((chunks, half, part, blk), BF16),
                pltpu.VMEM((chunks, na, part, blk), BF16),
                pltpu.VMEM((chunks, na, part, blk), BF16),
                pltpu.VMEM((chunks, na - 1, part, blk), BF16),
                pltpu.VMEM((chunks, na - 1, part, blk), BF16),
                pltpu.VMEM((rows, width), BF16),
                pltpu.VMEM((nb, blk), BF16),
                pltpu.VMEM((msg, blk), F32),
                pltpu.SMEM(gate_i.shape, jnp.int32),
                pltpu.SMEM(up_i.shape, jnp.int32),
                pltpu.SMEM(down_i.shape, jnp.int32),
                pltpu.SMEM((3, 1, 3), jnp.int32),
                pltpu.VMEM((8, 128), jnp.int32),
                pltpu.SMEM((8, 128), jnp.int32),
                dma((4,)),
                dma((2,)),
                dma((3, 3)),
                dma(()),
                dma((na - 1,)),
                dma((na - 1,)),
                dma((na,)),
                dma((na,)),
                dma((2 * na,)),
                dma((2 * na,)),
                dma((chunks,)),
                dma((chunks,)),
                dma((chunks,)),
                dma((chunks,)),
                dma((chunks, na - 1)),
                dma((chunks, na - 1)),
            ],
            compiler_params=pltpu.CompilerParams(
                collective_id=0, has_side_effects=True, vmem_limit_bytes=56 * 2**20
            ),
        )(
            tokens,
            norm_gain.reshape(nb, blk),
            curve_point,
            gate_i,
            up_i,
            down_i,
            jnp.transpose(counts, (0, 2, 1)),
            gate_t,
            up_t,
            down_t,
        )

    return jax.shard_map(
        shards,
        mesh=mesh,
        in_specs=(
            P(("group", "hid"), None),
            P(),
            P(),
            P(None, "hid", None, None, None),
            P(None, "hid", None, None, None),
            P(None, "hid", None, None, None),
            P(None, "hid", None),
            P(None, "hid", None),
            P(None, "hid", None),
            P(None, None, "hid"),
        ),
        out_specs=P(("group", "hid"), None),
        check_vma=False,
    )
```
